128 devices in a mesh: src: 8 (over z_lo, y), dst: 16 (over z_hi, x, core).
Axes of the slice: x: 4, y: 4, z: 4 (z_hi: 2, z_lo: 2; z = z_hi * 2 + z_lo), core: 2. Of those that a mesh axis runs over, the one named last changes fastest.
Arguments:
- section: bfloat16 [128, 256, 2048], P(('src', 'dst')), may hold values from -6 to 6
- leaf_maps: bfloat16 [128, 2, 256, 256], P(('src', 'dst')), may hold values from -0.375 to 0.375
- segment_maps: bfloat16 [128, 7, 4, 256, 256], P(('src', 'dst')), may hold values from -0.1875 to 0.1875
- final_maps: bfloat16 [128, 2, 256, 256], P(('src', 'dst')), may hold values from -0.25 to 0.25
Outputs:
- image: bfloat16 [2048, 128, 256], P(('src', 'dst'))
The draws below stay inside these ranges and needn't reach their ends.
All inputs are finite; a program needn't handle non-finite values.
Results may differ from the reference program's by a relative error of at most 0.02.
Values may be sent and summed in bfloat16 or wider, within the bound.
A program may use at most 64 MiB of HBM per device.

```python
import jax
import jax.numpy as jnp

CHEB = 256
SAMPLES = 256
OUTS = 256
PAIRS = 2048
BOXES = 128
SEGMENTS = 7


def levels(stream_key, extent, split, least, high):
    def one(dim, blocks):
        heights = jax.random.uniform(jax.random.fold_in(jax.random.fold_in(stream_key, 6), dim), (blocks,), jnp.float32, least / len(split), high / len(split))
        return jnp.repeat(jnp.exp(heights), extent[dim] // blocks).reshape((-1,) + (1,) * (len(extent) - dim - 1))

    loudness = one(*split[0])
    for cut in split[1:]:
        loudness = loudness * one(*cut)
    return loudness


def gaussian(key, dims, deviation, most, pieces=(), held_as=jnp.bfloat16):
    drawn = jax.random.normal(key, dims, jnp.float32) * deviation
    if len(pieces) > 0:
        drawn = levels(key, dims, pieces, -0.22, 0.18) * drawn
    return jnp.clip(drawn, min=-most, max=most).astype(held_as)


def setup_inputs(seed: int = 0) -> dict:
    seeds = jax.random.split(jax.random.key(seed), 5)
    return {
        "section": gaussian(seeds[0], (BOXES, SAMPLES, PAIRS), 1.0, 6.0, ((0, 128),)),
        "leaf_maps": gaussian(seeds[1], (BOXES, 2, CHEB, SAMPLES), SAMPLES ** -0.5, 0.375, ((0, 128),)),
        "segment_maps": gaussian(seeds[2], (BOXES, SEGMENTS, 4, CHEB, CHEB), (4 * CHEB) ** -0.5, 0.1875, ((0, 128),)),
        "final_maps": gaussian(seeds[3], (BOXES, 2, OUTS, CHEB), (2 * CHEB) ** -0.5, 0.25, ((0, 128),)),
    }


def reference(section, leaf_maps, segment_maps, final_maps):
    data = section.astype(jnp.float32)
    leaf = leaf_maps.astype(jnp.float32)
    weights = jnp.einsum("bcrs,bsp->bcrp", leaf, data).astype(jnp.bfloat16)
    boxes = jnp.arange(BOXES, dtype=jnp.int32)
    for segment in range(SEGMENTS):
        partner = jnp.bitwise_xor(boxes, jnp.int32(1 << segment))
        maps = segment_maps[:, segment].astype(jnp.float32)
        own_re = weights[:, 0].astype(jnp.float32)
        own_im = weights[:, 1].astype(jnp.float32)
        other = weights[partner]
        par_re = other[:, 0].astype(jnp.float32)
        par_im = other[:, 1].astype(jnp.float32)
        a_re, a_im, b_re, b_im = maps[:, 0], maps[:, 1], maps[:, 2], maps[:, 3]
        form = "bij,bjp->bip"
        new_re = (jnp.einsum(form, a_re, own_re) - jnp.einsum(form, a_im, own_im)
                  + jnp.einsum(form, b_re, par_re) - jnp.einsum(form, b_im, par_im))
        new_im = (jnp.einsum(form, a_re, own_im) + jnp.einsum(form, a_im, own_re)
                  + jnp.einsum(form, b_re, par_im) + jnp.einsum(form, b_im, par_re))
        weights = jnp.stack([new_re, new_im], axis=1).astype(jnp.bfloat16)
    final = final_maps.astype(jnp.float32)
    vals_re = weights[:, 0].astype(jnp.float32)
    vals_im = weights[:, 1].astype(jnp.float32)
    result = jnp.einsum("bor,brp->pbo", final[:, 0], vals_re) - jnp.einsum("bor,brp->pbo", final[:, 1], vals_im)
    return result.astype(jnp.bfloat16)
```

```python
import functools

import jax
import jax.numpy as jnp
from jax import lax
from jax.experimental import pallas as pl
from jax.experimental.pallas import tpu as pltpu
from jax.sharding import PartitionSpec as P

MESH = pl.DeviceIdType.MESH
CHUNK = 128
DIRECT = 2
LAGS = (0, 1, 2, 3, 4, 5, 6, 7)


def flip(index, bit):
    return index + (1 - 2 * ((index // bit) % 2)) * bit


def complex_step(own_maps, other_maps, own, other):
    both = jnp.dot(own_maps, own, preferred_element_type=jnp.float32)
    both = both + jnp.dot(other_maps, other, preferred_element_type=jnp.float32)
    half = both.shape[0] // 2
    upper, lower = both[:half], both[half:]
    real = upper[:, :CHUNK] - lower[:, CHUNK:]
    imag = upper[:, CHUNK:] + lower[:, :CHUNK]
    return jnp.concatenate([real, imag], axis=1).astype(jnp.bfloat16)


def fold_final(final, maps):
    half = maps.shape[0] // 2
    beside = jnp.concatenate([maps[:half], maps[half:]], axis=1)
    both = jnp.dot(final, beside, preferred_element_type=jnp.float32)
    real = both[:half, :half] - both[half:, half:]
    imag = both[:half, half:] + both[half:, :half]
    return jnp.concatenate([real.T, imag.T], axis=1).astype(jnp.bfloat16)


def kernel(
    chunks,
    section_any, leaf_any, segments_any, final_any,
    out,
    section, leaf, segments, final,
    w0, w1, w2, w2x, w3, w4, w5, w5y,
    r0, r1, r2, r3, r4, r5,
    x_maps, y_maps, own_fold, cross_fold, z_fold, kept, cross, r6,
    load_sem, send_sem, recv_sem, map_send, map_recv,
):
    src = lax.axis_index("src")
    dst = lax.axis_index("dst")
    core = (src, flip(dst, 1))
    x_near = (src, flip(dst, 2))
    x_far = (src, flip(dst, 4))
    x_back = (src, flip(flip(dst, 2), 4))
    z_far = (src, flip(dst, 8))
    y_near = (flip(src, 1), dst)
    y_back = (flip(flip(src, 1), 2), dst)
    z_near = (flip(src, 4), dst)
    partners = (core, x_near, x_far, x_back, z_far, y_near, y_back, z_near)

    loads = [
        pltpu.make_async_copy(section_any, section, load_sem.at[0]),
        pltpu.make_async_copy(leaf_any, leaf, load_sem.at[1]),
        pltpu.make_async_copy(final_any, final, load_sem.at[2]),
    ]
    loads += [
        pltpu.make_async_copy(segments_any.at[k], segments.at[k], load_sem.at[3 + k])
        for k in range(7)
    ]
    for load in loads:
        load.start()

    barrier = pltpu.get_barrier_semaphore()
    for partner in partners:
        pl.semaphore_signal(barrier, inc=1, device_id=partner, device_id_type=MESH)
    pl.semaphore_wait(barrier, len(partners))

    def remote(source, target, send, recv, partner):
        return pltpu.make_async_remote_copy(
            src_ref=source, dst_ref=target, send_sem=send, recv_sem=recv,
            device_id=partner, device_id_type=MESH,
        )

    def exchange(stage, source, target, chunk, partner):
        return remote(
            source.at[chunk], target.at[chunk],
            send_sem.at[stage], recv_sem.at[stage, chunk], partner,
        )

    x_map_copy = remote(segments_any.at[1], x_maps, map_send.at[0], map_recv.at[0], x_near)
    y_map_copy = remote(segments_any.at[4], y_maps, map_send.at[1], map_recv.at[1], y_near)
    z_map_copy = remote(cross_fold, z_fold, map_send.at[2], map_recv.at[2], z_near)
    y_map_copy.start()

    def at_step(step, stage, body):
        chunk = step - LAGS[stage]

        @pl.when((chunk >= 0) & (chunk < chunks))
        def _():
            body(chunk)

    def step_body(step, carry):
        def leaves(chunk):
            @pl.when(chunk == 0)
            def _():
                loads[0].wait()
                loads[1].wait()

            columns = pl.ds(pl.multiple_of(chunk * CHUNK, CHUNK), CHUNK)
            both = jnp.dot(leaf[...], section[:, columns], preferred_element_type=jnp.float32)
            half = both.shape[0] // 2
            w0[chunk] = jnp.concatenate([both[:half], both[half:]], axis=1).astype(jnp.bfloat16)
            exchange(0, w0, r0, chunk, core).start()

        def first(chunk):
            @pl.when(chunk == 0)
            def _():
                loads[3].wait()

            exchange(0, w0, r0, chunk, core).wait_recv()
            w1[chunk] = complex_step(segments[0, 0], segments[0, 1], w0[chunk], r0[chunk])
            exchange(1, w1, r1, chunk, x_near).start()

        def second(chunk):
            @pl.when(chunk == 0)
            def _():
                loads[4].wait()

            exchange(1, w1, r1, chunk, x_near).wait_recv()

            @pl.when(chunk >= DIRECT)
            def _():
                @pl.when(chunk == DIRECT)
                def _():
                    x_map_copy.wait_recv()

                w2x[chunk] = complex_step(x_maps[0], x_maps[1], r1[chunk], w1[chunk])
                exchange(2, w2x, r2, chunk, x_back).start()

            w2[chunk] = complex_step(segments[1, 0], segments[1, 1], w1[chunk], r1[chunk])

            @pl.when(chunk < DIRECT)
            def _():
                exchange(2, w2, r2, chunk, x_far).start()

            @pl.when(chunk == max(DIRECT - 1, 0))
            def _():
                if DIRECT > 0:
                    x_map_copy.start()

        def third(chunk):
            @pl.when(chunk == 0)
            def _():
                loads[5].wait()

            exchange(2, w2x, r2, chunk, x_back).wait_recv()
            w3[chunk] = complex_step(segments[2, 0], segments[2, 1], w2[chunk], r2[chunk])
            exchange(3, w3, r3, chunk, z_far).start()

        def fourth(chunk):
            @pl.when(chunk == 0)
            def _():
                loads[6].wait()

            exchange(3, w3, r3, chunk, z_far).wait_recv()
            w4[chunk] = complex_step(segments[3, 0], segments[3, 1], w3[chunk], r3[chunk])
            exchange(4, w4, r4, chunk, y_near).start()

        def fifth(chunk):
            @pl.when(chunk == 0)
            def _():
                loads[7].wait()
                y_map_copy.wait_recv()

            exchange(4, w4, r4, chunk, y_near).wait_recv()
            w5y[chunk] = complex_step(y_maps[0], y_maps[1], r4[chunk], w4[chunk])
            exchange(5, w5y, r5, chunk, y_back).start()
            w5[chunk] = complex_step(segments[4, 0], segments[4, 1], w4[chunk], r4[chunk])

        def sixth(chunk):
            @pl.when(chunk == 0)
            def _():
                loads[8].wait()
                z_map_copy.wait_recv()

            exchange(5, w5y, r5, chunk, y_back).wait_recv()
            last = complex_step(segments[5, 0], segments[5, 1], w5[chunk], r5[chunk]).T
            half = last.shape[1]
            both = jnp.dot(last, z_fold[...], preferred_element_type=jnp.float32)
            cross[chunk] = (both[:CHUNK, :half] - both[CHUNK:, half:]).astype(jnp.bfloat16)
            exchange(6, cross, r6, chunk, z_near).start()
            both = jnp.dot(last, own_fold[...], preferred_element_type=jnp.float32)
            kept[chunk] = both[:CHUNK, :half] - both[CHUNK:, half:]

        def seventh(chunk):
            exchange(6, cross, r6, chunk, z_near).wait_recv()
            out[chunk] = (kept[chunk] + r6[chunk].astype(jnp.float32)).astype(jnp.bfloat16)

        @pl.when(step == 1)
        def _():
            loads[2].wait()
            loads[9].wait()
            cross_fold[...] = fold_final(final[...], segments[6, 1])
            z_map_copy.start()
            own_fold[...] = fold_final(final[...], segments[6, 0])

        bodies = (leaves, first, second, third, fourth, fifth, sixth, seventh)
        for stage, body in enumerate(bodies):
            at_step(step, stage, body)
        return carry

    if DIRECT == 0:
        x_map_copy.start()
    lax.fori_loop(0, chunks + LAGS[-1], step_body, 0)

    def all_sent(stage, source, target, partner):
        remote(source, target, send_sem.at[stage], recv_sem.at[stage, 0], partner).wait_send()

    all_sent(0, w0, r0, core)
    all_sent(1, w1, r1, x_near)
    all_sent(2, w2x, r2, x_back)
    all_sent(3, w3, r3, z_far)
    all_sent(4, w4, r4, y_near)
    all_sent(5, w5y, r5, y_back)
    all_sent(6, cross, r6, z_near)
    x_map_copy.wait_send()
    y_map_copy.wait_send()
    z_map_copy.wait_send()


def butterfly(section, leaf, segments, final):
    samples, pairs = section.shape
    cheb = leaf.shape[0] // 2
    outs = final.shape[0] // 2
    chunks = pairs // CHUNK
    bf16 = jnp.bfloat16
    weights = pltpu.VMEM((chunks, cheb, 2 * CHUNK), bf16)
    image = pltpu.VMEM((chunks, CHUNK, outs), bf16)
    maps = pltpu.VMEM(segments.shape[1:], bf16)
    fold = pltpu.VMEM((cheb, 2 * outs), bf16)
    return pl.pallas_call(
        functools.partial(kernel, chunks),
        out_shape=jax.ShapeDtypeStruct((chunks, CHUNK, outs), bf16),
        in_specs=[pl.BlockSpec(memory_space=pl.ANY)] * 4,
        out_specs=pl.BlockSpec(memory_space=pltpu.VMEM),
        scratch_shapes=[
            pltpu.VMEM(section.shape, bf16),
            pltpu.VMEM(leaf.shape, bf16),
            pltpu.VMEM(segments.shape, bf16),
            pltpu.VMEM(final.shape, bf16),
        ]
        + [weights] * 14
        + [maps] * 2
        + [fold] * 3
        + [pltpu.VMEM((chunks, CHUNK, outs), jnp.float32), image, image]
        + [
            pltpu.SemaphoreType.DMA((10,)),
            pltpu.SemaphoreType.DMA((7,)),
            pltpu.SemaphoreType.DMA((7, chunks)),
            pltpu.SemaphoreType.DMA((3,)),
            pltpu.SemaphoreType.DMA((3,)),
        ],
        compiler_params=pltpu.CompilerParams(
            collective_id=0, has_side_effects=True, vmem_limit_bytes=56 << 20
        ),
        name="butterfly",
    )(section, leaf, segments, final)


def shards(section, leaf_maps, segment_maps, final_maps):
    _, _, cheb, samples = leaf_maps.shape
    outs = final_maps.shape[2]
    steps = segment_maps.shape[1]
    image = butterfly(
        section[0],
        leaf_maps.reshape(2 * cheb, samples),
        segment_maps.reshape(steps, 2, 2 * cheb, cheb),
        final_maps.reshape(2 * outs, cheb),
    )
    whole = image.reshape(section.shape[2], 1, outs)
    return lax.all_to_all(whole, ("src", "dst"), split_axis=0, concat_axis=1, tiled=True)


def solution(mesh):
    in_specs = (
        P(("src", "dst"), None, None),
        P(("src", "dst"), None, None, None),
        P(("src", "dst"), None, None, None, None),
        P(("src", "dst"), None, None, None),
    )
    out_specs = P(("src", "dst"), None, None)
    return jax.shard_map(shards, mesh=mesh, in_specs=in_specs, out_specs=out_specs, check_vma=False)
```

```python
import functools

import jax
import jax.numpy as jnp
from jax import lax
from jax.experimental import pallas as pl
from jax.experimental.pallas import tpu as pltpu
from jax.sharding import PartitionSpec as P

MESH = pl.DeviceIdType.MESH
CHUNK = 128
DIRECT = 2
LAGS = (0, 1, 2, 3, 5, 6, 7, 8)


def flip(index, bit):
    return index + (1 - 2 * ((index // bit) % 2)) * bit


def complex_step(own_maps, other_maps, own, other):
    both = jnp.dot(own_maps, own, preferred_element_type=jnp.float32)
    both = both + jnp.dot(other_maps, other, preferred_element_type=jnp.float32)
    half = both.shape[0] // 2
    upper, lower = both[:half], both[half:]
    real = upper[:, :CHUNK] - lower[:, CHUNK:]
    imag = upper[:, CHUNK:] + lower[:, :CHUNK]
    return jnp.concatenate([real, imag], axis=1).astype(jnp.bfloat16)


def fold_final(final, maps):
    half = maps.shape[0] // 2
    beside = jnp.concatenate([maps[:half], maps[half:]], axis=1)
    both = jnp.dot(final, beside, preferred_element_type=jnp.float32)
    real = both[:half, :half] - both[half:, half:]
    imag = both[:half, half:] + both[half:, :half]
    return jnp.concatenate([real.T, imag.T], axis=1).astype(jnp.bfloat16)


def kernel(
    chunks,
    section_any, leaf_any, segments_any, final_any,
    out,
    section, leaf, segments, final,
    w0, w1, w2, w2x, w3, w4, w5, w5y,
    r0, r1, r2, r3, r4, r5,
    x_maps, y_maps, own_fold, cross_fold, z_fold, kept, cross, r6, image, gathered,
    load_sem, send_sem, recv_sem, map_send, map_recv, own_sem, out_send, out_recv,
):
    src = lax.axis_index("src")
    dst = lax.axis_index("dst")
    columns_of_mesh = lax.axis_size("dst")
    box = src * columns_of_mesh + dst
    boxes, rows, outs = gathered.shape
    pieces = CHUNK // rows
    core = (src, flip(dst, 1))
    x_near = (src, flip(dst, 2))
    x_far = (src, flip(dst, 4))
    x_back = (src, flip(flip(dst, 2), 4))
    z_far = (src, flip(dst, 8))
    y_near = (flip(src, 1), dst)
    y_back = (flip(flip(src, 1), 2), dst)
    z_near = (flip(src, 4), dst)
    partners = (core, x_near, x_far, x_back, z_far, y_near, y_back, z_near)

    loads = [
        pltpu.make_async_copy(section_any, section, load_sem.at[0]),
        pltpu.make_async_copy(leaf_any, leaf, load_sem.at[1]),
        pltpu.make_async_copy(final_any, final, load_sem.at[2]),
    ]
    loads += [
        pltpu.make_async_copy(segments_any.at[k], segments.at[k], load_sem.at[3 + k])
        for k in range(7)
    ]
    for load in loads:
        load.start()

    barrier = pltpu.get_barrier_semaphore()
    for partner in partners:
        pl.semaphore_signal(barrier, inc=1, device_id=partner, device_id_type=MESH)
    pl.semaphore_wait(barrier, len(partners))

    def remote(source, target, send, recv, partner):
        return pltpu.make_async_remote_copy(
            src_ref=source, dst_ref=target, send_sem=send, recv_sem=recv,
            device_id=partner, device_id_type=MESH,
        )

    def exchange(stage, source, target, chunk, partner):
        return remote(
            source.at[chunk], target.at[chunk],
            send_sem.at[stage], recv_sem.at[stage, chunk], partner,
        )

    x_map_copy = remote(segments_any.at[1], x_maps, map_send.at[0], map_recv.at[0], x_near)
    y_map_copy = remote(segments_any.at[4], y_maps, map_send.at[1], map_recv.at[1], y_near)
    z_map_copy = remote(cross_fold, z_fold, map_send.at[2], map_recv.at[2], z_near)
    y_map_copy.start()

    def at_step(step, stage, body):
        chunk = step - LAGS[stage]

        @pl.when((chunk >= 0) & (chunk < chunks))
        def _():
            body(chunk)

    def step_body(step, carry):
        def leaves(chunk):
            @pl.when(chunk == 0)
            def _():
                loads[0].wait()
                loads[1].wait()

            columns = pl.ds(pl.multiple_of(chunk * CHUNK, CHUNK), CHUNK)
            both = jnp.dot(leaf[...], section[:, columns], preferred_element_type=jnp.float32)
            half = both.shape[0] // 2
            w0[chunk] = jnp.concatenate([both[:half], both[half:]], axis=1).astype(jnp.bfloat16)
            exchange(0, w0, r0, chunk, core).start()

        def first(chunk):
            @pl.when(chunk == 0)
            def _():
                loads[3].wait()

            exchange(0, w0, r0, chunk, core).wait_recv()
            w1[chunk] = complex_step(segments[0, 0], segments[0, 1], w0[chunk], r0[chunk])
            exchange(1, w1, r1, chunk, x_near).start()

        def second(chunk):
            @pl.when(chunk == 0)
            def _():
                loads[4].wait()

            exchange(1, w1, r1, chunk, x_near).wait_recv()

            @pl.when(chunk >= DIRECT)
            def _():
                @pl.when(chunk == DIRECT)
                def _():
                    x_map_copy.wait_recv()

                w2x[chunk] = complex_step(x_maps[0], x_maps[1], r1[chunk], w1[chunk])
                exchange(2, w2x, r2, chunk, x_back).start()

            w2[chunk] = complex_step(segments[1, 0], segments[1, 1], w1[chunk], r1[chunk])

            @pl.when(chunk < DIRECT)
            def _():
                exchange(2, w2, r2, chunk, x_far).start()

            @pl.when(chunk == max(DIRECT - 1, 0))
            def _():
                if DIRECT > 0:
                    x_map_copy.start()

        def third(chunk):
            @pl.when(chunk == 0)
            def _():
                loads[5].wait()

            exchange(2, w2x, r2, chunk, x_back).wait_recv()
            w3[chunk] = complex_step(segments[2, 0], segments[2, 1], w2[chunk], r2[chunk])
            exchange(3, w3, r3, chunk, z_far).start()

        def fourth(chunk):
            @pl.when(chunk == 0)
            def _():
                loads[6].wait()

            exchange(3, w3, r3, chunk, z_far).wait_recv()
            w4[chunk] = complex_step(segments[3, 0], segments[3, 1], w3[chunk], r3[chunk])
            exchange(4, w4, r4, chunk, y_near).start()

        def fifth(chunk):
            @pl.when(chunk == 0)
            def _():
                loads[7].wait()
                y_map_copy.wait_recv()

            exchange(4, w4, r4, chunk, y_near).wait_recv()
            w5y[chunk] = complex_step(y_maps[0], y_maps[1], r4[chunk], w4[chunk])
            exchange(5, w5y, r5, chunk, y_back).start()
            w5[chunk] = complex_step(segments[4, 0], segments[4, 1], w4[chunk], r4[chunk])

        def sixth(chunk):
            @pl.when(chunk == 0)
            def _():
                loads[8].wait()
                z_map_copy.wait_recv()

            exchange(5, w5y, r5, chunk, y_back).wait_recv()
            last = complex_step(segments[5, 0], segments[5, 1], w5[chunk], r5[chunk]).T
            half = last.shape[1]
            both = jnp.dot(last, z_fold[...], preferred_element_type=jnp.float32)
            cross[chunk] = (both[:CHUNK, :half] - both[CHUNK:, half:]).astype(jnp.bfloat16)
            exchange(6, cross, r6, chunk, z_near).start()
            both = jnp.dot(last, own_fold[...], preferred_element_type=jnp.float32)
            kept[chunk] = both[:CHUNK, :half] - both[CHUNK:, half:]

        def seventh(chunk):
            exchange(6, cross, r6, chunk, z_near).wait_recv()
            image[chunk] = (kept[chunk] + r6[chunk].astype(jnp.float32)).astype(jnp.bfloat16)

        @pl.when(step == 1)
        def _():
            loads[2].wait()
            loads[9].wait()
            cross_fold[...] = fold_final(final[...], segments[6, 1])
            z_map_copy.start()
            own_fold[...] = fold_final(final[...], segments[6, 0])

        bodies = (leaves, first, second, third, fourth, fifth, sixth, seventh)
        for stage, body in enumerate(bodies):
            at_step(step, stage, body)

        def deliver(turn, carry):
            chunk = step - LAGS[-1] - turn

            @pl.when((chunk >= 0) & (chunk < chunks))
            def _():
                piece = (turn + box) % pieces
                owner = chunk * pieces + piece
                start = pl.multiple_of(piece * rows, rows)
                part = image.at[chunk, pl.ds(start, rows)]

                @pl.when(owner == box)
                def _():
                    pltpu.make_async_copy(part, gathered.at[box], own_sem).start()

                @pl.when(owner != box)
                def _():
                    place = (owner // columns_of_mesh, owner % columns_of_mesh)
                    remote(part, gathered.at[box], out_send, out_recv, place).start()

            return carry

        lax.fori_loop(0, pieces, deliver, 0)
        return carry

    if DIRECT == 0:
        x_map_copy.start()
    lax.fori_loop(0, chunks + LAGS[-1] + pieces - 1, step_body, 0)

    others = gathered.at[pl.ds(0, boxes - 1)]
    everyone = remote(others, others, out_send, out_recv, core)
    everyone.wait_recv()
    pltpu.make_async_copy(gathered.at[0], gathered.at[0], own_sem).wait()
    side = rows * rows
    row = lax.broadcasted_iota(jnp.int32, (side, side), 0)
    column = lax.broadcasted_iota(jnp.int32, (side, side), 1)
    swap = jnp.where(column == (row % rows) * rows + row // rows, 1.0, 0.0).astype(jnp.bfloat16)
    for group in range(boxes // rows):
        span = pl.ds(group * rows, rows)
        block = gathered[span].reshape(side, outs)
        turned = jnp.dot(swap, block, preferred_element_type=jnp.float32).astype(jnp.bfloat16)
        out[:, span, :] = turned.reshape(rows, rows, outs)
    everyone.wait_send()

    def all_sent(stage, source, target, partner):
        remote(source, target, send_sem.at[stage], recv_sem.at[stage, 0], partner).wait_send()

    all_sent(0, w0, r0, core)
    all_sent(1, w1, r1, x_near)
    all_sent(2, w2x, r2, x_back)
    all_sent(3, w3, r3, z_far)
    all_sent(4, w4, r4, y_near)
    all_sent(5, w5y, r5, y_back)
    all_sent(6, cross, r6, z_near)
    x_map_copy.wait_send()
    y_map_copy.wait_send()
    z_map_copy.wait_send()


def butterfly(section, leaf, segments, final):
    samples, pairs = section.shape
    boxes = lax.axis_size("src") * lax.axis_size("dst")
    rows = pairs // boxes
    cheb = leaf.shape[0] // 2
    outs = final.shape[0] // 2
    chunks = pairs // CHUNK
    bf16 = jnp.bfloat16
    weights = pltpu.VMEM((chunks, cheb, 2 * CHUNK), bf16)
    image = pltpu.VMEM((chunks, CHUNK, outs), bf16)
    maps = pltpu.VMEM(segments.shape[1:], bf16)
    fold = pltpu.VMEM((cheb, 2 * outs), bf16)
    return pl.pallas_call(
        functools.partial(kernel, chunks),
        out_shape=jax.ShapeDtypeStruct((rows, boxes, outs), bf16),
        in_specs=[pl.BlockSpec(memory_space=pl.ANY)] * 4,
        out_specs=pl.BlockSpec(memory_space=pltpu.VMEM),
        scratch_shapes=[
            pltpu.VMEM(section.shape, bf16),
            pltpu.VMEM(leaf.shape, bf16),
            pltpu.VMEM(segments.shape, bf16),
            pltpu.VMEM(final.shape, bf16),
        ]
        + [weights] * 14
        + [maps] * 2
        + [fold] * 3
        + [pltpu.VMEM((chunks, CHUNK, outs), jnp.float32), image, image, image]
        + [pltpu.VMEM((boxes, rows, outs), bf16)]
        + [
            pltpu.SemaphoreType.DMA((10,)),
            pltpu.SemaphoreType.DMA((7,)),
            pltpu.SemaphoreType.DMA((7, chunks)),
            pltpu.SemaphoreType.DMA((3,)),
            pltpu.SemaphoreType.DMA((3,)),
            pltpu.SemaphoreType.DMA,
            pltpu.SemaphoreType.DMA,
            pltpu.SemaphoreType.DMA,
        ],
        compiler_params=pltpu.CompilerParams(
            collective_id=0, has_side_effects=True, vmem_limit_bytes=56 << 20
        ),
        name="butterfly",
    )(section, leaf, segments, final)


def shards(section, leaf_maps, segment_maps, final_maps):
    _, _, cheb, samples = leaf_maps.shape
    outs = final_maps.shape[2]
    steps = segment_maps.shape[1]
    return butterfly(
        section[0],
        leaf_maps.reshape(2 * cheb, samples),
        segment_maps.reshape(steps, 2, 2 * cheb, cheb),
        final_maps.reshape(2 * outs, cheb),
    )


def solution(mesh):
    in_specs = (
        P(("src", "dst"), None, None),
        P(("src", "dst"), None, None, None),
        P(("src", "dst"), None, None, None, None),
        P(("src", "dst"), None, None, None),
    )
    out_specs = P(("src", "dst"), None, None)
    return jax.shard_map(shards, mesh=mesh, in_specs=in_specs, out_specs=out_specs, check_vma=False)
```

```python
import functools

import jax
import jax.numpy as jnp
from jax import lax
from jax.experimental import pallas as pl
from jax.experimental.pallas import tpu as pltpu
from jax.sharding import PartitionSpec as P

MESH = pl.DeviceIdType.MESH
CHUNK = 128
LAGS = (0, 1, 3, 5, 8, 10, 12, 14)
SPACING = 1


def flip(index, bit):
    return index + (1 - 2 * ((index // bit) % 2)) * bit


def complex_maps(own_maps, other_maps):
    return jnp.concatenate([own_maps, other_maps], axis=1)


def combine(both):
    half = both.shape[0] // 2
    upper, lower = both[:half], both[half:]
    real = upper[:, :CHUNK] - lower[:, CHUNK:]
    imag = upper[:, CHUNK:] + lower[:, :CHUNK]
    return jnp.concatenate([real, imag], axis=1).astype(jnp.bfloat16)


def complex_step(maps, own, other):
    weights = jnp.concatenate([own, other], axis=0)
    return combine(jnp.dot(maps, weights, preferred_element_type=jnp.float32))


def two_steps(maps, near_maps, own, other):
    weights = jnp.concatenate([own, other], axis=0)
    every = jnp.concatenate([maps, near_maps], axis=0)
    both = jnp.dot(every, weights, preferred_element_type=jnp.float32)
    half = both.shape[0] // 2
    return combine(both[:half]), combine(both[half:])


def tile_of(odd, part, piece):
    low = (piece + odd) % 2
    return low * 8 + piece * 2 + (low + part) % 2


def fill_marks(marks, rows):
    shape = (CHUNK, marks.shape[1])
    row = lax.broadcasted_iota(jnp.int32, shape, 0)
    column = lax.broadcasted_iota(jnp.int32, shape, 1)
    half = CHUNK // 2
    piece = (column % half) // rows
    odd = column // CHUNK
    tile = tile_of(odd, (column % CHUNK) // half, piece)
    spot = row // rows
    pair = (spot % 2) * 4 + (spot // 2 + 8 - piece - 2 * odd) % 4
    fits = row % rows == column % rows

    def fill(step, carry):
        start = pl.multiple_of(step * CHUNK, CHUNK)
        chosen = jnp.where(fits & (tile == step), pair, -1)
        marks[pl.ds(start, CHUNK), :] = chosen.astype(jnp.float32)
        return carry

    lax.fori_loop(0, marks.shape[0] // CHUNK, fill, 0)


def fold_final(final, maps):
    half = maps.shape[0] // 2
    beside = jnp.concatenate([maps[:half], maps[half:]], axis=1)
    both = jnp.dot(final, beside, preferred_element_type=jnp.float32)
    real = both[:half, :half] - both[half:, half:]
    imag = both[:half, half:] + both[half:, :half]
    return jnp.concatenate([real.T, imag.T], axis=1).astype(jnp.bfloat16)


def kernel(
    chunks,
    section_any, leaf_any, segments_any, final_any,
    out,
    section, leaf, segments, final,
    w0, w1, w2, w2x, w3, w4, w5, w5y,
    r0, r1, r2, r3, r4, r5,
    marks, x_maps, y_maps, own_fold, cross_fold, z_fold, kept, sent, r6, image, gathered,
    load_sem, send_sem, recv_sem, map_send, map_recv, own_sem, out_send, out_recv,
):
    src = lax.axis_index("src")
    dst = lax.axis_index("dst")
    sources = lax.axis_size("src")
    targets = lax.axis_size("dst")
    box = src * targets + dst
    _, half_boxes, rows, outs = gathered.shape
    half = CHUNK // 2
    pieces = half // rows
    z_lo = src // (sources // 2)
    z_hi = dst // (targets // 2)

    kept_part = (z_lo + z_hi) % 2
    spots = CHUNK // rows

    def owner_of(chunk, piece):
        odd = chunk % 2
        pair = chunk // 2
        tile = tile_of(odd, kept_part, piece)
        return tile * spots + (pair + piece + 2 * odd) % 4 * 2 + pair // 4

    core = (src, flip(dst, 1))
    x_near = (src, flip(dst, 2))
    x_back = (src, flip(flip(dst, 2), 4))
    z_far = (src, flip(dst, 8))
    y_near = (flip(src, 1), dst)
    y_back = (flip(flip(src, 1), 2), dst)
    z_near = (flip(src, 4), dst)
    partners = (core, x_near, x_back, z_far, y_near, y_back, z_near)

    loads = [
        pltpu.make_async_copy(section_any, section, load_sem.at[0]),
        pltpu.make_async_copy(leaf_any, leaf, load_sem.at[1]),
        pltpu.make_async_copy(final_any, final, load_sem.at[2]),
    ]
    loads += [
        pltpu.make_async_copy(segments_any.at[k], segments.at[k], load_sem.at[3 + k])
        for k in range(7)
    ]
    for load in loads:
        load.start()

    fill_marks(marks, rows)
    barrier = pltpu.get_barrier_semaphore()
    for partner in partners:
        pl.semaphore_signal(barrier, inc=1, device_id=partner, device_id_type=MESH)
    pl.semaphore_wait(barrier, len(partners))

    def remote(source, target, send, recv, partner):
        return pltpu.make_async_remote_copy(
            src_ref=source, dst_ref=target, send_sem=send, recv_sem=recv,
            device_id=partner, device_id_type=MESH,
        )

    def exchange(stage, source, target, chunk, partner):
        return remote(
            source.at[chunk], target.at[chunk],
            send_sem.at[stage], recv_sem.at[stage, chunk], partner,
        )

    x_map_copy = remote(segments_any.at[1], x_maps, map_send.at[0], map_recv.at[0], x_near)
    y_map_copy = remote(segments_any.at[4], y_maps, map_send.at[1], map_recv.at[1], y_near)
    z_map_copy = remote(cross_fold, z_fold, map_send.at[2], map_recv.at[2], z_near)
    x_map_copy.start()
    y_map_copy.start()

    def last_exchange(chunk):
        return remote(
            sent.at[chunk, 1 - kept_part], r6.at[chunk],
            send_sem.at[6], recv_sem.at[6, chunk], z_near,
        )

    def at_step(step, stage, body):
        chunk = step - LAGS[stage]

        @pl.when((chunk >= 0) & (chunk < chunks))
        def _():
            body(chunk)

    def step_body(step, carry):
        def leaves(chunk):
            @pl.when(chunk == 0)
            def _():
                loads[0].wait()
                loads[1].wait()

            @pl.when(chunk % 2 == 0)
            def _():
                pair = (chunk // 2).astype(jnp.float32)
                pick = jnp.where(marks[...] == pair, 1.0, 0.0).astype(jnp.bfloat16)
                picked = jnp.dot(section[...], pick, preferred_element_type=jnp.float32)
                both = jnp.dot(
                    leaf[...], picked.astype(jnp.bfloat16), preferred_element_type=jnp.float32
                ).astype(jnp.bfloat16)
                cheb = both.shape[0] // 2
                for odd in range(2):
                    columns = slice(odd * CHUNK, (odd + 1) * CHUNK)
                    w0[chunk + odd] = jnp.concatenate(
                        [both[:cheb, columns], both[cheb:, columns]], axis=1
                    )
                    exchange(0, w0, r0, chunk + odd, core).start()

        def first(chunk):
            @pl.when(chunk == 0)
            def _():
                loads[3].wait()

            exchange(0, w0, r0, chunk, core).wait_recv()
            maps = complex_maps(segments[0, 0], segments[0, 1])
            w1[chunk] = complex_step(maps, w0[chunk], r0[chunk])
            exchange(1, w1, r1, chunk, x_near).start()

        def second(chunk):
            @pl.when(chunk == 0)
            def _():
                loads[4].wait()
                x_map_copy.wait_recv()

            exchange(1, w1, r1, chunk, x_near).wait_recv()
            maps = complex_maps(segments[1, 0], segments[1, 1])
            near_maps = complex_maps(x_maps[1], x_maps[0])
            w2[chunk], w2x[chunk] = two_steps(maps, near_maps, w1[chunk], r1[chunk])
            exchange(2, w2x, r2, chunk, x_back).start()

        def third(chunk):
            @pl.when(chunk == 0)
            def _():
                loads[5].wait()

            exchange(2, w2x, r2, chunk, x_back).wait_recv()
            maps = complex_maps(segments[2, 0], segments[2, 1])
            w3[chunk] = complex_step(maps, w2[chunk], r2[chunk])
            exchange(3, w3, r3, chunk, z_far).start()

        def fourth(chunk):
            @pl.when(chunk == 0)
            def _():
                loads[6].wait()

            exchange(3, w3, r3, chunk, z_far).wait_recv()
            maps = complex_maps(segments[3, 0], segments[3, 1])
            w4[chunk] = complex_step(maps, w3[chunk], r3[chunk])
            exchange(4, w4, r4, chunk, y_near).start()

        def fifth(chunk):
            @pl.when(chunk == 0)
            def _():
                loads[7].wait()
                y_map_copy.wait_recv()

            exchange(4, w4, r4, chunk, y_near).wait_recv()
            maps = complex_maps(segments[4, 0], segments[4, 1])
            near_maps = complex_maps(y_maps[1], y_maps[0])
            w5[chunk], w5y[chunk] = two_steps(maps, near_maps, w4[chunk], r4[chunk])
            exchange(5, w5y, r5, chunk, y_back).start()

        def sixth(chunk):
            @pl.when(chunk == 0)
            def _():
                loads[8].wait()
                z_map_copy.wait_recv()

            exchange(5, w5y, r5, chunk, y_back).wait_recv()
            maps = complex_maps(segments[5, 0], segments[5, 1])
            last = complex_step(maps, w5[chunk], r5[chunk]).T
            folds = jnp.concatenate([own_fold[...], z_fold[...]], axis=1)
            both = jnp.dot(last, folds, preferred_element_type=jnp.float32)
            own = both[:CHUNK, :outs] - both[CHUNK:, outs : 2 * outs]
            cross = both[:CHUNK, 2 * outs : 3 * outs] - both[CHUNK:, 3 * outs :]
            for part in range(2):
                span = slice(part * half, (part + 1) * half)
                kept[chunk, part, 0] = own[span]
                kept[chunk, part, 1] = cross[span]
                sent[chunk, part, 0] = own[span].astype(jnp.bfloat16)
                sent[chunk, part, 1] = cross[span].astype(jnp.bfloat16)
            last_exchange(chunk).start()

        def seventh(chunk):
            last_exchange(chunk).wait_recv()
            own = kept[chunk, kept_part, 0] + r6[chunk, 1].astype(jnp.float32)
            near = kept[chunk, kept_part, 1] + r6[chunk, 0].astype(jnp.float32)
            image[chunk, z_lo] = own.astype(jnp.bfloat16)
            image[chunk, 1 - z_lo] = near.astype(jnp.bfloat16)

        @pl.when(step == 1)
        def _():
            loads[2].wait()
            loads[9].wait()
            cross_fold[...] = fold_final(final[...], segments[6, 1])
            z_map_copy.start()
            own_fold[...] = fold_final(final[...], segments[6, 0])

        bodies = (leaves, first, second, third, fourth, fifth, sixth, seventh)
        for stage, body in enumerate(bodies):
            at_step(step, stage, body)

        def deliver(turn, carry):
            chunk = step - LAGS[-1] - turn * SPACING

            @pl.when((chunk >= 0) & (chunk < chunks))
            def _():
                piece = (turn + box) % pieces
                owner = owner_of(chunk, piece)
                start = pl.multiple_of(piece * rows, rows)
                part = image.at[chunk, :, pl.ds(start, rows)]
                slot = gathered.at[:, box % half_boxes]

                @pl.when(owner == box)
                def _():
                    pltpu.make_async_copy(part, slot, own_sem).start()

                @pl.when(owner != box)
                def _():
                    place = (owner // targets, owner % targets)
                    remote(part, slot, out_send, out_recv, place).start()

            return carry

        lax.fori_loop(0, pieces, deliver, 0)
        return carry

    lax.fori_loop(0, chunks + LAGS[-1] + (pieces - 1) * SPACING, step_body, 0)

    others = gathered.at[:, pl.ds(0, half_boxes - 1)]
    everyone = remote(others, others, out_send, out_recv, core)
    everyone.wait_recv()
    pltpu.make_async_copy(gathered.at[:, 0], gathered.at[:, 0], own_sem).wait()
    side = rows * rows
    row = lax.broadcasted_iota(jnp.int32, (side, side), 0)
    column = lax.broadcasted_iota(jnp.int32, (side, side), 1)
    swap = jnp.where(column == (row % rows) * rows + row // rows, 1.0, 0.0).astype(jnp.bfloat16)
    for low in range(2):
        for group in range(half_boxes // rows):
            block = gathered[low, pl.ds(group * rows, rows)].reshape(side, outs)
            turned = jnp.dot(swap, block, preferred_element_type=jnp.float32)
            span = pl.ds(low * half_boxes + group * rows, rows)
            out[:, span, :] = turned.astype(jnp.bfloat16).reshape(rows, rows, outs)
    everyone.wait_send()

    def all_sent(stage, source, target, partner):
        remote(source, target, send_sem.at[stage], recv_sem.at[stage, 0], partner).wait_send()

    all_sent(0, w0, r0, core)
    all_sent(1, w1, r1, x_near)
    all_sent(2, w2x, r2, x_back)
    all_sent(3, w3, r3, z_far)
    all_sent(4, w4, r4, y_near)
    all_sent(5, w5y, r5, y_back)
    all_sent(6, r6, r6, z_near)
    x_map_copy.wait_send()
    y_map_copy.wait_send()
    z_map_copy.wait_send()


def butterfly(section, leaf, segments, final):
    samples, pairs = section.shape
    boxes = lax.axis_size("src") * lax.axis_size("dst")
    rows = pairs // boxes
    cheb = leaf.shape[0] // 2
    outs = final.shape[0] // 2
    chunks = pairs // CHUNK
    bf16 = jnp.bfloat16
    weights = pltpu.VMEM((chunks, cheb, 2 * CHUNK), bf16)
    image = pltpu.VMEM((chunks, 2, CHUNK // 2, outs), bf16)
    maps = pltpu.VMEM(segments.shape[1:], bf16)
    fold = pltpu.VMEM((cheb, 2 * outs), bf16)
    return pl.pallas_call(
        functools.partial(kernel, chunks),
        out_shape=jax.ShapeDtypeStruct((rows, boxes, outs), bf16),
        in_specs=[pl.BlockSpec(memory_space=pl.ANY)] * 4,
        out_specs=pl.BlockSpec(memory_space=pltpu.VMEM),
        scratch_shapes=[
            pltpu.VMEM(section.shape, bf16),
            pltpu.VMEM(leaf.shape, bf16),
            pltpu.VMEM(segments.shape, bf16),
            pltpu.VMEM(final.shape, bf16),
        ]
        + [weights] * 14
        + [pltpu.VMEM((pairs, 2 * CHUNK), jnp.float32)]
        + [maps] * 2
        + [fold] * 3
        + [pltpu.VMEM((chunks, 2, 2, CHUNK // 2, outs), jnp.float32)]
        + [pltpu.VMEM((chunks, 2, 2, CHUNK // 2, outs), bf16), image, image]
        + [pltpu.VMEM((2, boxes // 2, rows, outs), bf16)]
        + [
            pltpu.SemaphoreType.DMA((10,)),
            pltpu.SemaphoreType.DMA((7,)),
            pltpu.SemaphoreType.DMA((7, chunks)),
            pltpu.SemaphoreType.DMA((3,)),
            pltpu.SemaphoreType.DMA((3,)),
            pltpu.SemaphoreType.DMA,
            pltpu.SemaphoreType.DMA,
            pltpu.SemaphoreType.DMA,
        ],
        compiler_params=pltpu.CompilerParams(
            collective_id=0, has_side_effects=True, vmem_limit_bytes=56 << 20
        ),
        name="butterfly",
    )(section, leaf, segments, final)


def shards(section, leaf_maps, segment_maps, final_maps):
    _, _, cheb, samples = leaf_maps.shape
    outs = final_maps.shape[2]
    steps = segment_maps.shape[1]
    return butterfly(
        section[0],
        leaf_maps.reshape(2 * cheb, samples),
        segment_maps.reshape(steps, 2, 2 * cheb, cheb),
        final_maps.reshape(2 * outs, cheb),
    )


def solution(mesh):
    in_specs = (
        P(("src", "dst"), None, None),
        P(("src", "dst"), None, None, None),
        P(("src", "dst"), None, None, None, None),
        P(("src", "dst"), None, None, None),
    )
    out_specs = P(("src", "dst"), None, None)
    return jax.shard_map(shards, mesh=mesh, in_specs=in_specs, out_specs=out_specs, check_vma=False)
```

```python
import functools

import jax
import jax.numpy as jnp
from jax import lax
from jax.experimental import pallas as pl
from jax.experimental.pallas import tpu as pltpu
from jax.sharding import PartitionSpec as P

MESH = pl.DeviceIdType.MESH
CHUNK = 128
FIRST_STEP = (0, 1, 2, 4, 6, 8, 19, 22)
EIGHTHS = (1, 3, 8, 8, 8, 8, 3, 2)


def flip(index, bit):
    return index + (1 - 2 * ((index // bit) % 2)) * bit


def complex_maps(own_maps, other_maps):
    return jnp.concatenate([own_maps, other_maps], axis=1)


def combine(both):
    half = both.shape[0] // 2
    upper, lower = both[:half], both[half:]
    real = upper[:, :CHUNK] - lower[:, CHUNK:]
    imag = upper[:, CHUNK:] + lower[:, :CHUNK]
    return jnp.concatenate([real, imag], axis=1).astype(jnp.bfloat16)


def complex_step(maps, own, other):
    weights = jnp.concatenate([own, other], axis=0)
    return combine(jnp.dot(maps, weights, preferred_element_type=jnp.float32))


def two_steps(maps, near_maps, own, other):
    weights = jnp.concatenate([own, other], axis=0)
    every = jnp.concatenate([maps, near_maps], axis=0)
    both = jnp.dot(every, weights, preferred_element_type=jnp.float32)
    half = both.shape[0] // 2
    return combine(both[:half]), combine(both[half:])


def tile_of(odd, part, piece):
    low = (piece + odd) % 2
    return low * 8 + piece * 2 + (low + part) % 2


def fill_marks(marks, rows):
    shape = (CHUNK, marks.shape[1])
    row = lax.broadcasted_iota(jnp.int32, shape, 0)
    column = lax.broadcasted_iota(jnp.int32, shape, 1)
    half = CHUNK // 2
    piece = (column % half) // rows
    odd = column // CHUNK
    tile = tile_of(odd, (column % CHUNK) // half, piece)
    spot = row // rows
    pair = (spot % 2) * 4 + (spot // 2 + 8 - piece - 2 * odd) % 4
    fits = row % rows == column % rows

    def fill(step, carry):
        start = pl.multiple_of(step * CHUNK, CHUNK)
        chosen = jnp.where(fits & (tile == step), pair, -1)
        marks[pl.ds(start, CHUNK), :] = chosen.astype(jnp.float32)
        return carry

    lax.fori_loop(0, marks.shape[0] // CHUNK, fill, 0)


def fold_final(final, maps):
    half = maps.shape[0] // 2
    beside = jnp.concatenate([maps[:half], maps[half:]], axis=1)
    both = jnp.dot(final, beside, preferred_element_type=jnp.float32)
    real = both[:half, :half] - both[half:, half:]
    imag = both[:half, half:] + both[half:, :half]
    return jnp.concatenate([real.T, imag.T], axis=1).astype(jnp.bfloat16)


def kernel(
    chunks,
    section_any, leaf_any, segments_any, final_any,
    out,
    section, leaf, segments, final,
    w0, w1, w2, w2x, w3, w4, w5, w5y,
    r0, r1, r2, r3, r4, r5,
    marks, x_maps, y_maps, own_fold, cross_fold, z_fold, kept, sent, r6, image, gathered,
    load_sem, send_sem, recv_sem, map_send, map_recv, own_sem, out_send, out_recv,
):
    src = lax.axis_index("src")
    dst = lax.axis_index("dst")
    sources = lax.axis_size("src")
    targets = lax.axis_size("dst")
    box = src * targets + dst
    _, half_boxes, rows, outs = gathered.shape
    half = CHUNK // 2
    pieces = half // rows
    z_lo = src // (sources // 2)
    z_hi = dst // (targets // 2)

    kept_part = (z_lo + z_hi) % 2
    spots = CHUNK // rows

    def owner_of(chunk, piece):
        odd = chunk % 2
        pair = chunk // 2
        tile = tile_of(odd, kept_part, piece)
        return tile * spots + (pair + piece + 2 * odd) % 4 * 2 + pair // 4

    core = (src, flip(dst, 1))
    x_near = (src, flip(dst, 2))
    x_back = (src, flip(flip(dst, 2), 4))
    z_far = (src, flip(dst, 8))
    y_near = (flip(src, 1), dst)
    y_back = (flip(flip(src, 1), 2), dst)
    z_near = (flip(src, 4), dst)
    partners = (core, x_near, x_back, z_far, y_near, y_back, z_near)

    loads = [
        pltpu.make_async_copy(section_any, section, load_sem.at[0]),
        pltpu.make_async_copy(leaf_any, leaf, load_sem.at[1]),
        pltpu.make_async_copy(final_any, final, load_sem.at[2]),
    ]
    loads += [
        pltpu.make_async_copy(segments_any.at[k], segments.at[k], load_sem.at[3 + k])
        for k in range(7)
    ]
    for load in loads:
        load.start()

    fill_marks(marks, rows)
    barrier = pltpu.get_barrier_semaphore()
    for partner in partners:
        pl.semaphore_signal(barrier, inc=1, device_id=partner, device_id_type=MESH)
    pl.semaphore_wait(barrier, len(partners))

    def remote(source, target, send, recv, partner):
        return pltpu.make_async_remote_copy(
            src_ref=source, dst_ref=target, send_sem=send, recv_sem=recv,
            device_id=partner, device_id_type=MESH,
        )

    def exchange(stage, source, target, chunk, partner):
        return remote(
            source.at[chunk], target.at[chunk],
            send_sem.at[stage], recv_sem.at[stage, chunk], partner,
        )

    x_map_copy = remote(segments_any.at[1], x_maps, map_send.at[0], map_recv.at[0], x_near)
    y_map_copy = remote(segments_any.at[4], y_maps, map_send.at[1], map_recv.at[1], y_near)
    z_map_copy = remote(cross_fold, z_fold, map_send.at[2], map_recv.at[2], z_near)
    x_map_copy.start()
    y_map_copy.start()

    def last_exchange(chunk):
        return remote(
            sent.at[chunk, 1 - kept_part], r6.at[chunk],
            send_sem.at[6], recv_sem.at[6, chunk], z_near,
        )

    def done_before(step, stage):
        late = 8 * (step - FIRST_STEP[stage]) + EIGHTHS[stage] - 1
        return jnp.clip(jnp.maximum(late, 0) // EIGHTHS[stage], 0, chunks)

    def at_step(step, stage, body):
        def one(chunk, carry):
            body(chunk)
            return carry

        lax.fori_loop(done_before(step, stage), done_before(step + 1, stage), one, 0)

    def step_body(step, carry):
        def leaves(chunk):
            @pl.when(chunk == 0)
            def _():
                loads[0].wait()
                loads[1].wait()

            @pl.when(chunk % 2 == 0)
            def _():
                pair = (chunk // 2).astype(jnp.float32)
                pick = jnp.where(marks[...] == pair, 1.0, 0.0).astype(jnp.bfloat16)
                picked = jnp.dot(section[...], pick, preferred_element_type=jnp.float32)
                both = jnp.dot(
                    leaf[...], picked.astype(jnp.bfloat16), preferred_element_type=jnp.float32
                ).astype(jnp.bfloat16)
                cheb = both.shape[0] // 2
                for odd in range(2):
                    columns = slice(odd * CHUNK, (odd + 1) * CHUNK)
                    w0[chunk + odd] = jnp.concatenate(
                        [both[:cheb, columns], both[cheb:, columns]], axis=1
                    )
                    exchange(0, w0, r0, chunk + odd, core).start()

        def first(chunk):
            @pl.when(chunk == 0)
            def _():
                loads[3].wait()

            exchange(0, w0, r0, chunk, core).wait_recv()
            maps = complex_maps(segments[0, 0], segments[0, 1])
            w1[chunk] = complex_step(maps, w0[chunk], r0[chunk])
            exchange(1, w1, r1, chunk, x_near).start()

        def second(chunk):
            @pl.when(chunk == 0)
            def _():
                loads[4].wait()
                x_map_copy.wait_recv()

            exchange(1, w1, r1, chunk, x_near).wait_recv()
            maps = complex_maps(segments[1, 0], segments[1, 1])
            near_maps = complex_maps(x_maps[1], x_maps[0])
            w2[chunk], w2x[chunk] = two_steps(maps, near_maps, w1[chunk], r1[chunk])
            exchange(2, w2x, r2, chunk, x_back).start()

        def third(chunk):
            @pl.when(chunk == 0)
            def _():
                loads[5].wait()

            exchange(2, w2x, r2, chunk, x_back).wait_recv()
            maps = complex_maps(segments[2, 0], segments[2, 1])
            w3[chunk] = complex_step(maps, w2[chunk], r2[chunk])
            exchange(3, w3, r3, chunk, z_far).start()

        def fourth(chunk):
            @pl.when(chunk == 0)
            def _():
                loads[6].wait()

            exchange(3, w3, r3, chunk, z_far).wait_recv()
            maps = complex_maps(segments[3, 0], segments[3, 1])
            w4[chunk] = complex_step(maps, w3[chunk], r3[chunk])
            exchange(4, w4, r4, chunk, y_near).start()

        def fifth(chunk):
            @pl.when(chunk == 0)
            def _():
                loads[7].wait()
                y_map_copy.wait_recv()

            exchange(4, w4, r4, chunk, y_near).wait_recv()
            maps = complex_maps(segments[4, 0], segments[4, 1])
            near_maps = complex_maps(y_maps[1], y_maps[0])
            w5[chunk], w5y[chunk] = two_steps(maps, near_maps, w4[chunk], r4[chunk])
            exchange(5, w5y, r5, chunk, y_back).start()

        def sixth(chunk):
            @pl.when(chunk == 0)
            def _():
                loads[8].wait()
                z_map_copy.wait_recv()

            exchange(5, w5y, r5, chunk, y_back).wait_recv()
            maps = complex_maps(segments[5, 0], segments[5, 1])
            last = complex_step(maps, w5[chunk], r5[chunk]).T
            folds = jnp.concatenate([own_fold[...], z_fold[...]], axis=1)
            both = jnp.dot(last, folds, preferred_element_type=jnp.float32)
            own = both[:CHUNK, :outs] - both[CHUNK:, outs : 2 * outs]
            cross = both[:CHUNK, 2 * outs : 3 * outs] - both[CHUNK:, 3 * outs :]
            for part in range(2):
                span = slice(part * half, (part + 1) * half)
                kept[chunk, part, 0] = own[span]
                kept[chunk, part, 1] = cross[span]
                sent[chunk, part, 0] = own[span].astype(jnp.bfloat16)
                sent[chunk, part, 1] = cross[span].astype(jnp.bfloat16)
            last_exchange(chunk).start()

        def seventh(chunk):
            last_exchange(chunk).wait_recv()
            own = kept[chunk, kept_part, 0] + r6[chunk, 1].astype(jnp.float32)
            near = kept[chunk, kept_part, 1] + r6[chunk, 0].astype(jnp.float32)
            image[chunk, z_lo] = own.astype(jnp.bfloat16)
            image[chunk, 1 - z_lo] = near.astype(jnp.bfloat16)

            def deliver(turn, carry):
                piece = (turn + box) % pieces
                owner = owner_of(chunk, piece)
                start = pl.multiple_of(piece * rows, rows)
                part = image.at[chunk, :, pl.ds(start, rows)]
                slot = gathered.at[:, box % half_boxes]

                @pl.when(owner == box)
                def _():
                    pltpu.make_async_copy(part, slot, own_sem).start()

                @pl.when(owner != box)
                def _():
                    place = (owner // targets, owner % targets)
                    remote(part, slot, out_send, out_recv, place).start()

                return carry

            lax.fori_loop(0, pieces, deliver, 0)

        @pl.when(step == 1)
        def _():
            loads[2].wait()
            loads[9].wait()
            cross_fold[...] = fold_final(final[...], segments[6, 1])
            z_map_copy.start()
            own_fold[...] = fold_final(final[...], segments[6, 0])

        bodies = (leaves, first, second, third, fourth, fifth, sixth, seventh)
        for stage, body in enumerate(bodies):
            at_step(step, stage, body)

        return carry

    steps = FIRST_STEP[-1] + (chunks - 1) * EIGHTHS[-1] // 8 + 1
    lax.fori_loop(0, steps, step_body, 0)

    others = gathered.at[:, pl.ds(0, half_boxes - 1)]
    everyone = remote(others, others, out_send, out_recv, core)
    everyone.wait_recv()
    pltpu.make_async_copy(gathered.at[:, 0], gathered.at[:, 0], own_sem).wait()
    side = rows * rows
    row = lax.broadcasted_iota(jnp.int32, (side, side), 0)
    column = lax.broadcasted_iota(jnp.int32, (side, side), 1)
    swap = jnp.where(column == (row % rows) * rows + row // rows, 1.0, 0.0).astype(jnp.bfloat16)
    for low in range(2):
        for group in range(half_boxes // rows):
            block = gathered[low, pl.ds(group * rows, rows)].reshape(side, outs)
            turned = jnp.dot(swap, block, preferred_element_type=jnp.float32)
            span = pl.ds(low * half_boxes + group * rows, rows)
            out[:, span, :] = turned.astype(jnp.bfloat16).reshape(rows, rows, outs)
    everyone.wait_send()

    def all_sent(stage, source, target, partner):
        remote(source, target, send_sem.at[stage], recv_sem.at[stage, 0], partner).wait_send()

    all_sent(0, w0, r0, core)
    all_sent(1, w1, r1, x_near)
    all_sent(2, w2x, r2, x_back)
    all_sent(3, w3, r3, z_far)
    all_sent(4, w4, r4, y_near)
    all_sent(5, w5y, r5, y_back)
    all_sent(6, r6, r6, z_near)
    x_map_copy.wait_send()
    y_map_copy.wait_send()
    z_map_copy.wait_send()


def butterfly(section, leaf, segments, final):
    samples, pairs = section.shape
    boxes = lax.axis_size("src") * lax.axis_size("dst")
    rows = pairs // boxes
    cheb = leaf.shape[0] // 2
    outs = final.shape[0] // 2
    chunks = pairs // CHUNK
    bf16 = jnp.bfloat16
    weights = pltpu.VMEM((chunks, cheb, 2 * CHUNK), bf16)
    image = pltpu.VMEM((chunks, 2, CHUNK // 2, outs), bf16)
    maps = pltpu.VMEM(segments.shape[1:], bf16)
    fold = pltpu.VMEM((cheb, 2 * outs), bf16)
    return pl.pallas_call(
        functools.partial(kernel, chunks),
        out_shape=jax.ShapeDtypeStruct((rows, boxes, outs), bf16),
        in_specs=[pl.BlockSpec(memory_space=pl.ANY)] * 4,
        out_specs=pl.BlockSpec(memory_space=pltpu.VMEM),
        scratch_shapes=[
            pltpu.VMEM(section.shape, bf16),
            pltpu.VMEM(leaf.shape, bf16),
            pltpu.VMEM(segments.shape, bf16),
            pltpu.VMEM(final.shape, bf16),
        ]
        + [weights] * 14
        + [pltpu.VMEM((pairs, 2 * CHUNK), jnp.float32)]
        + [maps] * 2
        + [fold] * 3
        + [pltpu.VMEM((chunks, 2, 2, CHUNK // 2, outs), jnp.float32)]
        + [pltpu.VMEM((chunks, 2, 2, CHUNK // 2, outs), bf16), image, image]
        + [pltpu.VMEM((2, boxes // 2, rows, outs), bf16)]
        + [
            pltpu.SemaphoreType.DMA((10,)),
            pltpu.SemaphoreType.DMA((7,)),
            pltpu.SemaphoreType.DMA((7, chunks)),
            pltpu.SemaphoreType.DMA((3,)),
            pltpu.SemaphoreType.DMA((3,)),
            pltpu.SemaphoreType.DMA,
            pltpu.SemaphoreType.DMA,
            pltpu.SemaphoreType.DMA,
        ],
        compiler_params=pltpu.CompilerParams(
            collective_id=0, has_side_effects=True, vmem_limit_bytes=56 << 20
        ),
        name="butterfly",
    )(section, leaf, segments, final)


def shards(section, leaf_maps, segment_maps, final_maps):
    _, _, cheb, samples = leaf_maps.shape
    outs = final_maps.shape[2]
    steps = segment_maps.shape[1]
    return butterfly(
        section[0],
        leaf_maps.reshape(2 * cheb, samples),
        segment_maps.reshape(steps, 2, 2 * cheb, cheb),
        final_maps.reshape(2 * outs, cheb),
    )


def solution(mesh):
    in_specs = (
        P(("src", "dst"), None, None),
        P(("src", "dst"), None, None, None),
        P(("src", "dst"), None, None, None, None),
        P(("src", "dst"), None, None, None),
    )
    out_specs = P(("src", "dst"), None, None)
    return jax.shard_map(shards, mesh=mesh, in_specs=in_specs, out_specs=out_specs, check_vma=False)
```

```python
import functools

import jax
import jax.numpy as jnp
from jax import lax
from jax.experimental import pallas as pl
from jax.experimental.pallas import tpu as pltpu
from jax.sharding import PartitionSpec as P

MESH = pl.DeviceIdType.MESH
CHUNK = 128
FIRST_STEP = (0, 1, 2, 4, 6, 8, 19, 22)
EIGHTHS = (1, 3, 8, 8, 8, 8, 3, 2)


def flip(index, bit):
    return index + (1 - 2 * ((index // bit) % 2)) * bit


def complex_maps(own_maps, other_maps):
    return jnp.concatenate([own_maps, other_maps], axis=1)


def combine(both):
    half = both.shape[0] // 2
    upper, lower = both[:half], both[half:]
    real = upper[:, :CHUNK] - lower[:, CHUNK:]
    imag = upper[:, CHUNK:] + lower[:, :CHUNK]
    return jnp.concatenate([real, imag], axis=1).astype(jnp.bfloat16)


def complex_step(maps, own, other):
    weights = jnp.concatenate([own, other], axis=0)
    return combine(jnp.dot(maps, weights, preferred_element_type=jnp.float32))


def two_steps(maps, near_maps, own, other):
    weights = jnp.concatenate([own, other], axis=0)
    every = jnp.concatenate([maps, near_maps], axis=0)
    both = jnp.dot(every, weights, preferred_element_type=jnp.float32)
    half = both.shape[0] // 2
    return combine(both[:half]), combine(both[half:])


def tile_of(odd, part, piece):
    low = (piece + odd) % 2
    return low * 8 + piece * 2 + (low + part) % 2


def fill_marks(marks, rows):
    shape = (CHUNK, marks.shape[1])
    row = lax.broadcasted_iota(jnp.int32, shape, 0)
    column = lax.broadcasted_iota(jnp.int32, shape, 1)
    half = CHUNK // 2
    piece = (column % half) // rows
    odd = column // CHUNK
    tile = tile_of(odd, (column % CHUNK) // half, piece)
    spot = row // rows
    pair = (spot % 2) * 4 + (spot // 2 + 8 - piece - 2 * odd) % 4
    fits = row % rows == column % rows

    def fill(step, carry):
        start = pl.multiple_of(step * CHUNK, CHUNK)
        chosen = jnp.where(fits & (tile == step), pair, -1)
        marks[pl.ds(start, CHUNK), :] = chosen.astype(jnp.float32)
        return carry

    lax.fori_loop(0, marks.shape[0] // CHUNK, fill, 0)


def fold_final(final, maps):
    half = maps.shape[0] // 2
    beside = jnp.concatenate([maps[:half], maps[half:]], axis=1)
    both = jnp.dot(final, beside, preferred_element_type=jnp.float32)
    real = both[:half, :half] - both[half:, half:]
    imag = both[:half, half:] + both[half:, :half]
    return jnp.concatenate([real.T, imag.T], axis=1).astype(jnp.bfloat16)


def kernel(
    chunks,
    section_any, leaf_any, segments_any, final_any,
    out,
    section, leaf, segments, final,
    w0, w1, w2, w2x, w3, w4, w5, w5y,
    r0, r1, r2, r3, r4, r5,
    marks, x_maps, y_maps, own_fold, cross_fold, z_fold, kept, sent, r6, image, gathered,
    load_sem, send_sem, recv_sem, map_send, map_recv, own_sem, out_send, out_recv,
):
    src = lax.axis_index("src")
    dst = lax.axis_index("dst")
    sources = lax.axis_size("src")
    targets = lax.axis_size("dst")
    box = src * targets + dst
    _, half_boxes, rows, outs = gathered.shape
    half = CHUNK // 2
    pieces = half // rows
    z_lo = src // (sources // 2)
    z_hi = dst // (targets // 2)

    kept_part = (z_lo + z_hi) % 2
    spots = CHUNK // rows

    def owner_of(chunk, piece):
        odd = chunk % 2
        pair = chunk // 2
        tile = tile_of(odd, kept_part, piece)
        return tile * spots + (pair + piece + 2 * odd) % 4 * 2 + pair // 4

    core = (src, flip(dst, 1))
    x_near = (src, flip(dst, 2))
    x_back = (src, flip(flip(dst, 2), 4))
    z_far = (src, flip(dst, 8))
    y_near = (flip(src, 1), dst)
    y_back = (flip(flip(src, 1), 2), dst)
    z_near = (flip(src, 4), dst)
    partners = (core, x_near, x_back, z_far, y_near, y_back, z_near)

    barrier = pltpu.get_barrier_semaphore()
    for partner in partners:
        pl.semaphore_signal(barrier, inc=1, device_id=partner, device_id_type=MESH)

    loads = [
        pltpu.make_async_copy(section_any, section, load_sem.at[0]),
        pltpu.make_async_copy(leaf_any, leaf, load_sem.at[1]),
        pltpu.make_async_copy(final_any, final, load_sem.at[2]),
    ]
    loads += [
        pltpu.make_async_copy(segments_any.at[k], segments.at[k], load_sem.at[3 + k])
        for k in range(7)
    ]
    for load in loads:
        load.start()

    pl.semaphore_wait(barrier, len(partners))

    def remote(source, target, send, recv, partner):
        return pltpu.make_async_remote_copy(
            src_ref=source, dst_ref=target, send_sem=send, recv_sem=recv,
            device_id=partner, device_id_type=MESH,
        )

    def exchange(stage, source, target, chunk, partner):
        return remote(
            source.at[chunk], target.at[chunk],
            send_sem.at[stage], recv_sem.at[stage, chunk], partner,
        )

    x_map_copy = remote(segments_any.at[1], x_maps, map_send.at[0], map_recv.at[0], x_near)
    y_map_copy = remote(segments_any.at[4], y_maps, map_send.at[1], map_recv.at[1], y_near)
    z_map_copy = remote(cross_fold, z_fold, map_send.at[2], map_recv.at[2], z_near)
    x_map_copy.start()
    y_map_copy.start()
    fill_marks(marks, rows)

    def last_exchange(chunk):
        return remote(
            sent.at[chunk, 1 - kept_part], r6.at[chunk],
            send_sem.at[6], recv_sem.at[6, chunk], z_near,
        )

    def done_before(step, stage):
        late = 8 * (step - FIRST_STEP[stage]) + EIGHTHS[stage] - 1
        return jnp.clip(jnp.maximum(late, 0) // EIGHTHS[stage], 0, chunks)

    def at_step(step, stage, body):
        def one(chunk, carry):
            body(chunk)
            return carry

        lax.fori_loop(done_before(step, stage), done_before(step + 1, stage), one, 0)

    def step_body(step, carry):
        def leaves(chunk):
            @pl.when(chunk == 0)
            def _():
                loads[0].wait()
                loads[1].wait()

            @pl.when(chunk % 2 == 0)
            def _():
                pair = (chunk // 2).astype(jnp.float32)
                pick = jnp.where(marks[...] == pair, 1.0, 0.0).astype(jnp.bfloat16)
                picked = jnp.dot(section[...], pick, preferred_element_type=jnp.float32)
                both = jnp.dot(
                    leaf[...], picked.astype(jnp.bfloat16), preferred_element_type=jnp.float32
                ).astype(jnp.bfloat16)
                cheb = both.shape[0] // 2
                for odd in range(2):
                    columns = slice(odd * CHUNK, (odd + 1) * CHUNK)
                    w0[chunk + odd] = jnp.concatenate(
                        [both[:cheb, columns], both[cheb:, columns]], axis=1
                    )
                    exchange(0, w0, r0, chunk + odd, core).start()

        def first(chunk):
            @pl.when(chunk == 0)
            def _():
                loads[3].wait()

            exchange(0, w0, r0, chunk, core).wait_recv()
            maps = complex_maps(segments[0, 0], segments[0, 1])
            w1[chunk] = complex_step(maps, w0[chunk], r0[chunk])
            exchange(1, w1, r1, chunk, x_near).start()

        def second(chunk):
            @pl.when(chunk == 0)
            def _():
                loads[4].wait()
                x_map_copy.wait_recv()

            exchange(1, w1, r1, chunk, x_near).wait_recv()
            maps = complex_maps(segments[1, 0], segments[1, 1])
            near_maps = complex_maps(x_maps[1], x_maps[0])
            w2[chunk], w2x[chunk] = two_steps(maps, near_maps, w1[chunk], r1[chunk])
            exchange(2, w2x, r2, chunk, x_back).start()

        def third(chunk):
            @pl.when(chunk == 0)
            def _():
                loads[5].wait()

            exchange(2, w2x, r2, chunk, x_back).wait_recv()
            maps = complex_maps(segments[2, 0], segments[2, 1])
            w3[chunk] = complex_step(maps, w2[chunk], r2[chunk])
            exchange(3, w3, r3, chunk, z_far).start()

        def fourth(chunk):
            @pl.when(chunk == 0)
            def _():
                loads[6].wait()

            exchange(3, w3, r3, chunk, z_far).wait_recv()
            maps = complex_maps(segments[3, 0], segments[3, 1])
            w4[chunk] = complex_step(maps, w3[chunk], r3[chunk])
            exchange(4, w4, r4, chunk, y_near).start()

        def fifth(chunk):
            @pl.when(chunk == 0)
            def _():
                loads[7].wait()
                y_map_copy.wait_recv()

            exchange(4, w4, r4, chunk, y_near).wait_recv()
            maps = complex_maps(segments[4, 0], segments[4, 1])
            near_maps = complex_maps(y_maps[1], y_maps[0])
            w5[chunk], w5y[chunk] = two_steps(maps, near_maps, w4[chunk], r4[chunk])
            exchange(5, w5y, r5, chunk, y_back).start()

        def sixth(chunk):
            @pl.when(chunk == 0)
            def _():
                loads[8].wait()
                z_map_copy.wait_recv()

            exchange(5, w5y, r5, chunk, y_back).wait_recv()
            maps = complex_maps(segments[5, 0], segments[5, 1])
            last = complex_step(maps, w5[chunk], r5[chunk]).T
            folds = jnp.concatenate([own_fold[...], z_fold[...]], axis=1)
            both = jnp.dot(last, folds, preferred_element_type=jnp.float32)
            own = both[:CHUNK, :outs] - both[CHUNK:, outs : 2 * outs]
            cross = both[:CHUNK, 2 * outs : 3 * outs] - both[CHUNK:, 3 * outs :]
            for part in range(2):
                span = slice(part * half, (part + 1) * half)
                kept[chunk, part, 0] = own[span]
                kept[chunk, part, 1] = cross[span]
                sent[chunk, part, 0] = own[span].astype(jnp.bfloat16)
                sent[chunk, part, 1] = cross[span].astype(jnp.bfloat16)
            last_exchange(chunk).start()

        def seventh(chunk):
            last_exchange(chunk).wait_recv()
            own = kept[chunk, kept_part, 0] + r6[chunk, 1].astype(jnp.float32)
            near = kept[chunk, kept_part, 1] + r6[chunk, 0].astype(jnp.float32)
            image[chunk, z_lo] = own.astype(jnp.bfloat16)
            image[chunk, 1 - z_lo] = near.astype(jnp.bfloat16)

            def deliver(turn, carry):
                piece = (turn + box) % pieces
                owner = owner_of(chunk, piece)
                start = pl.multiple_of(piece * rows, rows)
                part = image.at[chunk, :, pl.ds(start, rows)]
                slot = gathered.at[:, box % half_boxes]

                @pl.when(owner == box)
                def _():
                    pltpu.make_async_copy(part, slot, own_sem).start()

                @pl.when(owner != box)
                def _():
                    place = (owner // targets, owner % targets)
                    remote(part, slot, out_send, out_recv, place).start()

                return carry

            lax.fori_loop(0, pieces, deliver, 0)

        @pl.when(step == 1)
        def _():
            loads[2].wait()
            loads[9].wait()
            cross_fold[...] = fold_final(final[...], segments[6, 1])
            z_map_copy.start()
            own_fold[...] = fold_final(final[...], segments[6, 0])

        bodies = (leaves, first, second, third, fourth, fifth, sixth, seventh)
        for stage, body in enumerate(bodies):
            at_step(step, stage, body)

        return carry

    steps = FIRST_STEP[-1] + (chunks - 1) * EIGHTHS[-1] // 8 + 1
    lax.fori_loop(0, steps, step_body, 0)

    others = gathered.at[:, pl.ds(0, half_boxes - 1)]
    everyone = remote(others, others, out_send, out_recv, core)
    everyone.wait_recv()
    pltpu.make_async_copy(gathered.at[:, 0], gathered.at[:, 0], own_sem).wait()
    side = rows * rows
    row = lax.broadcasted_iota(jnp.int32, (side, side), 0)
    column = lax.broadcasted_iota(jnp.int32, (side, side), 1)
    swap = jnp.where(column == (row % rows) * rows + row // rows, 1.0, 0.0).astype(jnp.bfloat16)
    for low in range(2):
        for group in range(half_boxes // rows):
            block = gathered[low, pl.ds(group * rows, rows)].reshape(side, outs)
            turned = jnp.dot(swap, block, preferred_element_type=jnp.float32)
            span = pl.ds(low * half_boxes + group * rows, rows)
            out[:, span, :] = turned.astype(jnp.bfloat16).reshape(rows, rows, outs)
    everyone.wait_send()

    def all_sent(stage, source, target, partner):
        remote(source, target, send_sem.at[stage], recv_sem.at[stage, 0], partner).wait_send()

    all_sent(0, w0, r0, core)
    all_sent(1, w1, r1, x_near)
    all_sent(2, w2x, r2, x_back)
    all_sent(3, w3, r3, z_far)
    all_sent(4, w4, r4, y_near)
    all_sent(5, w5y, r5, y_back)
    all_sent(6, r6, r6, z_near)
    x_map_copy.wait_send()
    y_map_copy.wait_send()
    z_map_copy.wait_send()


def butterfly(section, leaf, segments, final):
    samples, pairs = section.shape
    boxes = lax.axis_size("src") * lax.axis_size("dst")
    rows = pairs // boxes
    cheb = leaf.shape[0] // 2
    outs = final.shape[0] // 2
    chunks = pairs // CHUNK
    bf16 = jnp.bfloat16
    weights = pltpu.VMEM((chunks, cheb, 2 * CHUNK), bf16)
    image = pltpu.VMEM((chunks, 2, CHUNK // 2, outs), bf16)
    maps = pltpu.VMEM(segments.shape[1:], bf16)
    fold = pltpu.VMEM((cheb, 2 * outs), bf16)
    return pl.pallas_call(
        functools.partial(kernel, chunks),
        out_shape=jax.ShapeDtypeStruct((rows, boxes, outs), bf16),
        in_specs=[pl.BlockSpec(memory_space=pl.ANY)] * 4,
        out_specs=pl.BlockSpec(memory_space=pltpu.VMEM),
        scratch_shapes=[
            pltpu.VMEM(section.shape, bf16),
            pltpu.VMEM(leaf.shape, bf16),
            pltpu.VMEM(segments.shape, bf16),
            pltpu.VMEM(final.shape, bf16),
        ]
        + [weights] * 14
        + [pltpu.VMEM((pairs, 2 * CHUNK), jnp.float32)]
        + [maps] * 2
        + [fold] * 3
        + [pltpu.VMEM((chunks, 2, 2, CHUNK // 2, outs), jnp.float32)]
        + [pltpu.VMEM((chunks, 2, 2, CHUNK // 2, outs), bf16), image, image]
        + [pltpu.VMEM((2, boxes // 2, rows, outs), bf16)]
        + [
            pltpu.SemaphoreType.DMA((10,)),
            pltpu.SemaphoreType.DMA((7,)),
            pltpu.SemaphoreType.DMA((7, chunks)),
            pltpu.SemaphoreType.DMA((3,)),
            pltpu.SemaphoreType.DMA((3,)),
            pltpu.SemaphoreType.DMA,
            pltpu.SemaphoreType.DMA,
            pltpu.SemaphoreType.DMA,
        ],
        compiler_params=pltpu.CompilerParams(
            collective_id=0, has_side_effects=True, vmem_limit_bytes=56 << 20
        ),
        name="butterfly",
    )(section, leaf, segments, final)


def shards(section, leaf_maps, segment_maps, final_maps):
    _, _, cheb, samples = leaf_maps.shape
    outs = final_maps.shape[2]
    steps = segment_maps.shape[1]
    return butterfly(
        section[0],
        leaf_maps.reshape(2 * cheb, samples),
        segment_maps.reshape(steps, 2, 2 * cheb, cheb),
        final_maps.reshape(2 * outs, cheb),
    )


def solution(mesh):
    in_specs = (
        P(("src", "dst"), None, None),
        P(("src", "dst"), None, None, None),
        P(("src", "dst"), None, None, None, None),
        P(("src", "dst"), None, None, None),
    )
    out_specs = P(("src", "dst"), None, None)
    return jax.shard_map(shards, mesh=mesh, in_specs=in_specs, out_specs=out_specs, check_vma=False)
```
